32 devices in a mesh: depth: 4 (over x, core), trans: 8 (over z, y).
Axes of the slice: x: 2, y: 2, z: 4, core: 2. Of those that a mesh axis runs over, the one named last changes fastest.
Arguments:
- screens: float32 [4, 2048, 2048], P('depth', 'trans'), may hold values from -1.5 to 1.5
- measured: bfloat16 [1, 2, 2048, 2048], P(None, None, 'trans'), may hold values from -4 to 4
- angle_index: int32 [1, 2], replicated, may hold values from -128 to 128
Outputs:
- screen_grad: float32 [4, 2048, 2048], P('depth', 'trans')
The draws below stay inside these ranges and needn't reach their ends.
All inputs are finite; a program needn't handle non-finite values.
Results may differ from the reference program's by a relative error of at most 0.0003.
Values sent between devices are 32-bit elements; how exact they have to be, the bound alone decides.
A program may use at most 256 MiB of HBM per device.

```python
import math
import jax
import jax.numpy as jnp
from jax import lax

N = 2048
ANGLES = 1
SLICES = 4
N_TRANS = 8


def block_levels(key, shape, split, least, high):
    def one(position, shards_of):
        heights = jax.random.uniform(jax.random.fold_in(jax.random.fold_in(key, 6), position), (shards_of,), jnp.float32, least / len(split), high / len(split))
        return jnp.repeat(jnp.exp(heights), shape[position] // shards_of).reshape((-1,) + (1,) * (len(shape) - position - 1))

    loudness = one(*split[0])
    for cut in split[1:]:
        loudness = loudness * one(*cut)
    return loudness


def centred(own_key, shape, scale, reach, cuts=(), held_as=jnp.bfloat16):
    array = scale * jax.random.normal(own_key, shape, jnp.float32)
    if cuts:
        array = array * block_levels(own_key, shape, cuts, -0.22, 0.18)
    return jnp.clip(array, -reach, reach).astype(held_as)


def setup_inputs(seed: int = 0) -> dict:
    streams_of = jax.random.split(jax.random.key(seed), 4)
    return {
        "screens": jnp.clip(jax.random.uniform(streams_of[0], (SLICES, N, N), jnp.float32, -1.5, 1.5) * block_levels(streams_of[0], (SLICES, N, N), ((0, 4), (1, 8)), -0.4, 0.0), -1.5, 1.5),
        "measured": centred(streams_of[1], (ANGLES, 2, N, N), 0.7, 4.0, ((2, 8),)),
        "angle_index": jax.random.randint(streams_of[2], (ANGLES, 2), 0 - N // 16, N // 16 + 1).astype(jnp.int32),
    }


TWO_PI = 2.0 * math.pi


def dft_table(length_all):
    positions = jnp.arange(length_all, dtype=jnp.int32)
    turn_count = (positions[:, None] * positions[None, :]) % length_all
    radians = (-TWO_PI / length_all) * turn_count.astype(jnp.float32)
    return jnp.cos(radians), jnp.sin(radians)


def line_factors(outer_grid, inner_grid, outer_size, length_all, orientation):
    twist = (-TWO_PI / length_all) * ((inner_grid * outer_grid) % length_all).astype(jnp.float32)
    frequency = outer_grid + outer_size * inner_grid
    signed_freq = jnp.where(frequency < length_all // 2, frequency, frequency - length_all)
    spread = (-orientation * TWO_PI / (8 * length_all)) * ((signed_freq * signed_freq) % (8 * length_all)).astype(jnp.float32)
    return jnp.cos(twist), jnp.sin(twist), jnp.cos(spread), jnp.sin(spread)


def complex_product(layout_spec, left_pair, right_pair):
    def product_of(left_part, right_part):
        return jnp.einsum(layout_spec, left_part.astype(jnp.float32), right_part.astype(jnp.float32), precision=lax.Precision.HIGHEST)
    real_part = product_of(left_pair[0], right_pair[0]) - product_of(left_pair[1], right_pair[1])
    imag_part = product_of(left_pair[0], right_pair[1]) + product_of(left_pair[1], right_pair[0])
    return real_part, imag_part


def times_phase(complex_pair, cosine, sine_part):
    real_part = complex_pair[0] * cosine - complex_pair[1] * sine_part
    imag_part = complex_pair[0] * sine_part + complex_pair[1] * cosine
    return real_part, imag_part


def line_pass(wave_field, layout_spec, outer_size, inner_size, outer_grid, inner_grid, orientation):
    length_all = outer_size * inner_size
    outer_table = dft_table(outer_size)
    inner_table = dft_table(inner_size)
    twist_cos, twist_sin, spread_cos, spread_sin = line_factors(outer_grid, inner_grid, outer_size, length_all, orientation)
    spec_k = layout_spec.replace("p", "k")
    spec_m = spec_k.replace("q", "m")
    complex_pair = (wave_field[0], wave_field[1])
    complex_pair = complex_product(layout_spec + ",pk->" + spec_k, complex_pair, outer_table)
    complex_pair = times_phase(complex_pair, twist_cos, twist_sin)
    complex_pair = complex_product(spec_k + ",qm->" + spec_m, complex_pair, inner_table)
    complex_pair = times_phase(complex_pair, spread_cos, spread_sin)
    complex_pair = complex_product(spec_m + ",mq->" + spec_k, complex_pair, (inner_table[0], -inner_table[1]))
    complex_pair = times_phase(complex_pair, twist_cos, -twist_sin)
    complex_pair = complex_product(spec_k + ",kp->" + layout_spec, complex_pair, (outer_table[0], -outer_table[1]))
    return jnp.stack((complex_pair[0] / length_all, complex_pair[1] / length_all))


def x_pass(wave_field, orientation):
    old_shape = wave_field.shape
    inner_size = min(128, N)
    outer_size = N // inner_size
    outer_grid = lax.broadcasted_iota(jnp.int32, (outer_size, inner_size), 0)
    inner_grid = lax.broadcasted_iota(jnp.int32, (outer_size, inner_size), 1)
    shaped = wave_field.reshape(old_shape[:3] + (outer_size, inner_size))
    result = line_pass(shaped, "brpq", outer_size, inner_size, outer_grid, inner_grid, orientation)
    return result.reshape(old_shape)


def y_pass(wave_field, orientation):
    old_shape = wave_field.shape
    outer_size = N_TRANS
    inner_size = N // N_TRANS
    outer_grid = lax.broadcasted_iota(jnp.int32, (outer_size, inner_size, 1), 0)
    inner_grid = lax.broadcasted_iota(jnp.int32, (outer_size, inner_size, 1), 1)
    shaped = wave_field.reshape(old_shape[:2] + (outer_size, inner_size, old_shape[3]))
    result = line_pass(shaped, "bpqc", outer_size, inner_size, outer_grid, inner_grid, orientation)
    return result.reshape(old_shape)


def illumination(tilt_table, row_start, row_count, grid_cells):
    row_index = row_start + lax.broadcasted_iota(jnp.int32, (row_count, grid_cells), 0)
    column_index = lax.broadcasted_iota(jnp.int32, (row_count, grid_cells), 1)
    turn_count = (tilt_table[:, 0][:, None, None] * column_index + tilt_table[:, 1][:, None, None] * row_index) % grid_cells
    radians = (TWO_PI / grid_cells) * turn_count.astype(jnp.float32)
    return jnp.stack((jnp.cos(radians), jnp.sin(radians)))


def rotate(wave_field, cosine, sine_part):
    real_part = wave_field[0] * cosine - wave_field[1] * sine_part
    imag_part = wave_field[0] * sine_part + wave_field[1] * cosine
    return jnp.stack((real_part, imag_part))


def rotate_back(wave_field, cosine, sine_part):
    real_part = wave_field[0] * cosine + wave_field[1] * sine_part
    imag_part = wave_field[1] * cosine - wave_field[0] * sine_part
    return jnp.stack((real_part, imag_part))


def grad_term(adjoint, kept_field):
    term = adjoint[1] * kept_field[0] - adjoint[0] * kept_field[1]
    return jnp.sum(term, axis=0)


def reference(screens, measured, angle_index):
    wave_field = illumination(angle_index, 0, N, N)
    kept_fields = []
    for slice_at in range(SLICES):
        wave_field = rotate(wave_field, jnp.cos(screens[slice_at]), jnp.sin(screens[slice_at]))
        kept_fields.append(wave_field)
        wave_field = y_pass(x_pass(wave_field, 1.0), 1.0)
    target = jnp.moveaxis(measured, 1, 0)
    adjoint = wave_field - target.astype(jnp.float32)
    gradients = [None] * SLICES
    for slice_at in reversed(range(SLICES)):
        adjoint = x_pass(y_pass(adjoint, -1.0), -1.0)
        gradients[slice_at] = grad_term(adjoint, kept_fields[slice_at])
        adjoint = rotate_back(adjoint, jnp.cos(screens[slice_at]), jnp.sin(screens[slice_at]))
    return jnp.stack(gradients)
```

```python
import functools
import math

import jax
import jax.numpy as jnp
import numpy as np
from jax import lax
from jax.experimental import pallas as pl
from jax.experimental.pallas import tpu as pltpu
from jax.sharding import PartitionSpec as P

TWO_PI = 2.0 * math.pi
LANES = 128
AXES = ("trans", "depth")


def as_pair(table):
    high = np.asarray(table, np.float32).astype(jnp.bfloat16)
    low = (np.asarray(table, np.float64) - high.astype(np.float64)).astype(jnp.bfloat16)
    return high, low


def tables_of(cells):
    outer = cells // LANES
    at = np.arange(LANES)
    radians = -TWO_PI / LANES * (at[:, None] * at[None, :] % LANES)
    c, s = np.cos(radians), np.sin(radians)
    ahead = np.block([[c, s], [-s, c]])
    back = np.block([[c, -s], [s, c]])
    k = np.arange(outer)[:, None]
    twist = -TWO_PI / cells * (k * at[None, :] % cells)
    freq = k + outer * at[None, :]
    signed = np.where(freq < cells // 2, freq, freq - cells)
    spread = -TWO_PI / (8 * cells) * (signed * signed % (8 * cells))
    phases = np.stack(
        [np.cos(twist), np.sin(twist), np.cos(spread) / cells, np.sin(spread) / cells]
    ).astype(np.float32)
    dft = np.stack([*as_pair(ahead), *as_pair(back)])
    return dft, phases


def small_dft(parts, sign):
    count = len(parts)
    if count == 1:
        return parts
    even = small_dft(parts[0::2], sign)
    odd = small_dft(parts[1::2], sign)
    low, high = [], []
    for k in range(count // 2):
        (er, ei), (r, i) = even[k], odd[k]
        turn = 8 * k / count
        if turn == 2:
            r, i = (-i, r) if sign > 0 else (i, -r)
        elif turn == 1:
            h = math.sqrt(0.5)
            r, i = (h * (r - sign * i), h * (i + sign * r))
        elif turn == 3:
            h = math.sqrt(0.5)
            r, i = (-h * (r + sign * i), h * (sign * r - i))
        elif k:
            c, s = math.cos(TWO_PI * k / count), sign * math.sin(TWO_PI * k / count)
            r, i = (r * c - i * s, r * s + i * c)
        low.append((er + r, ei + i))
        high.append((er - r, ei - i))
    return low + high


def product(value, dft_ref, high):
    top = value.astype(jnp.bfloat16)
    rest = (value - top.astype(jnp.float32)).astype(jnp.bfloat16)
    dot = functools.partial(jnp.dot, preferred_element_type=jnp.float32)
    return dot(top, dft_ref[high]) + (dot(top, dft_ref[high + 1]) + dot(rest, dft_ref[high]))


def chunk_pass(re, im, dft_ref, phase_ref, sign):
    lines, cells = re.shape
    outer = cells // LANES
    cut = [slice(LANES * a, LANES * (a + 1)) for a in range(outer)]
    parts = small_dft([(re[:, c], im[:, c]) for c in cut], -1)
    rows = []
    for k, (r, i) in enumerate(parts):
        c, s = phase_ref[0, k : k + 1], phase_ref[1, k : k + 1]
        rows.append(jnp.concatenate([r * c - i * s, r * s + i * c], 1))
    z = product(jnp.concatenate(rows, 0), dft_ref, 0)
    rows = []
    for k in range(outer):
        r, i = z[lines * k : lines * (k + 1), :LANES], z[lines * k : lines * (k + 1), LANES:]
        c, s = phase_ref[2, k : k + 1], sign * phase_ref[3, k : k + 1]
        rows.append(jnp.concatenate([r * c - i * s, r * s + i * c], 1))
    z = product(jnp.concatenate(rows, 0), dft_ref, 2)
    parts = []
    for k in range(outer):
        r, i = z[lines * k : lines * (k + 1), :LANES], z[lines * k : lines * (k + 1), LANES:]
        c, s = phase_ref[0, k : k + 1], phase_ref[1, k : k + 1]
        parts.append((r * c + i * s, i * c - r * s))
    parts = small_dft(parts, 1)
    return jnp.concatenate([p[0] for p in parts], 1), jnp.concatenate([p[1] for p in parts], 1)


def pass_kernel(sign, x_ref, dft_ref, phase_ref, out_ref):
    lines = x_ref.shape[1]
    step = min(16, lines)

    @pl.loop(0, lines // step)
    def _(at):
        here = pl.ds(pl.multiple_of(at * step, step), step)
        re, im = chunk_pass(x_ref[0, here], x_ref[1, here], dft_ref, phase_ref, sign)
        out_ref[0, here] = re
        out_ref[1, here] = im


def line_pass(field, tables, sign):
    whole = pl.BlockSpec(memory_space=pltpu.VMEM)
    return pl.pallas_call(
        functools.partial(pass_kernel, sign),
        out_shape=jax.ShapeDtypeStruct(field.shape, jnp.float32),
        in_specs=[whole] * 3,
        out_specs=whole,
        compiler_params=pltpu.CompilerParams(vmem_limit_bytes=32 << 20),
        name="line_pass",
    )(field, *tables)


def turn(field):
    two, lines, cells = field.shape
    count = cells // lines
    blocks = field.reshape(two * lines, cells).T.reshape(count, lines, two * lines)
    blocks = lax.all_to_all(blocks, AXES, split_axis=0, concat_axis=0, tiled=True)
    blocks = blocks.reshape(count, lines, two, lines)
    return blocks.transpose(2, 1, 0, 3).reshape(two, lines, cells)


def rotate(field, cosine, sine):
    return jnp.stack((field[0] * cosine - field[1] * sine, field[0] * sine + field[1] * cosine))


def illumination(angle_index, first, lines, cells):
    def wave(positions, tilt):
        turns = lax.rem(lax.rem(positions * tilt, cells) + cells, cells)
        radians = TWO_PI / cells * turns.astype(jnp.float32)
        return jnp.cos(radians), jnp.sin(radians)

    column = wave(jnp.arange(cells, dtype=jnp.int32), angle_index[0, 0])
    row = wave(first + jnp.arange(lines, dtype=jnp.int32), angle_index[0, 1])
    cc, cs = column[0][None], column[1][None]
    rc, rs = row[0][:, None], row[1][:, None]
    return jnp.stack((cc * rc - cs * rs, cc * rs + cs * rc))


def on_device(screens, measured, angle_index):
    depth_count = lax.axis_size("depth")
    held, cells = screens.shape[1:]
    lines = held // depth_count
    depth_at = lax.axis_index("depth")
    first = lax.axis_index("trans") * held + depth_at * lines
    tables = [jnp.asarray(t) for t in tables_of(cells)]

    spread_out = screens.reshape(depth_count, lines, cells)
    own = lax.all_to_all(spread_out, "depth", split_axis=0, concat_axis=0, tiled=True)
    odd = turn(own[1::2])
    phase = [odd[g // 2] if g % 2 else own[g] for g in range(depth_count)]
    cosine, sine = [jnp.cos(p) for p in phase], [jnp.sin(p) for p in phase]

    field = illumination(angle_index, first, lines, cells)
    kept = []
    for g in range(depth_count):
        field = rotate(field, cosine[g], sine[g])
        kept.append(field)
        field = line_pass(turn(line_pass(field, tables, 1.0)), tables, 1.0)
    target = lax.dynamic_slice_in_dim(measured[0], depth_at * lines, lines, 1)
    field = field - target.astype(jnp.float32)
    grads = [None] * depth_count
    for g in reversed(range(depth_count)):
        field = line_pass(turn(line_pass(field, tables, -1.0)), tables, -1.0)
        grads[g] = field[1] * kept[g][0] - field[0] * kept[g][1]
        field = rotate(field, cosine[g], -sine[g])
    odd = turn(jnp.stack(grads[1::2]))
    rows = jnp.stack([odd[g // 2] if g % 2 else grads[g] for g in range(depth_count)])
    out = lax.all_to_all(rows, "depth", split_axis=0, concat_axis=0, tiled=True)
    return out.reshape(1, held, cells)


def solution(mesh):
    placed = (P("depth", "trans", None), P(None, None, "trans", None), P())
    return jax.shard_map(
        on_device, mesh=mesh, in_specs=placed, out_specs=P("depth", "trans", None), check_vma=False
    )
```

```python
import functools
import math

import jax
import jax.numpy as jnp
import numpy as np
from jax import lax
from jax.experimental import pallas as pl
from jax.experimental.pallas import tpu as pltpu
from jax.sharding import PartitionSpec as P

TWO_PI = 2.0 * math.pi
LANES = 128


def as_pair(table):
    high = np.asarray(table, np.float32).astype(jnp.bfloat16)
    low = (np.asarray(table, np.float64) - high.astype(np.float64)).astype(jnp.bfloat16)
    return high, low


def tables_of(cells):
    outer = cells // LANES
    at = np.arange(LANES)
    radians = -TWO_PI / LANES * (at[:, None] * at[None, :] % LANES)
    c, s = np.cos(radians), np.sin(radians)
    ahead = np.block([[c, s], [-s, c]])
    back = np.block([[c, -s], [s, c]])
    k = np.arange(outer)[:, None]
    twist = -TWO_PI / cells * (k * at[None, :] % cells)
    freq = k + outer * at[None, :]
    signed = np.where(freq < cells // 2, freq, freq - cells)
    spread = -TWO_PI / (8 * cells) * (signed * signed % (8 * cells))
    phases = np.stack(
        [np.cos(twist), np.sin(twist), np.cos(spread) / cells, np.sin(spread) / cells]
    ).astype(np.float32)
    dft = np.stack([*as_pair(ahead), *as_pair(back)])
    return dft, phases


def small_dft(parts, sign):
    count = len(parts)
    if count == 1:
        return parts
    even = small_dft(parts[0::2], sign)
    odd = small_dft(parts[1::2], sign)
    low, high = [], []
    for k in range(count // 2):
        (er, ei), (r, i) = even[k], odd[k]
        turn = 8 * k / count
        if turn == 2:
            r, i = (-i, r) if sign > 0 else (i, -r)
        elif turn == 1:
            h = math.sqrt(0.5)
            r, i = (h * (r - sign * i), h * (i + sign * r))
        elif turn == 3:
            h = math.sqrt(0.5)
            r, i = (-h * (r + sign * i), h * (sign * r - i))
        elif k:
            c, s = math.cos(TWO_PI * k / count), sign * math.sin(TWO_PI * k / count)
            r, i = (r * c - i * s, r * s + i * c)
        low.append((er + r, ei + i))
        high.append((er - r, ei - i))
    return low + high


def product(value, dft_ref, high):
    top = value.astype(jnp.bfloat16)
    rest = (value - top.astype(jnp.float32)).astype(jnp.bfloat16)
    dot = functools.partial(jnp.dot, preferred_element_type=jnp.float32)
    return dot(top, dft_ref[high]) + (dot(top, dft_ref[high + 1]) + dot(rest, dft_ref[high]))


def chunk_pass(re, im, dft_ref, phase_ref, sign):
    lines, cells = re.shape
    outer = cells // LANES
    cut = [slice(LANES * a, LANES * (a + 1)) for a in range(outer)]
    parts = small_dft([(re[:, c], im[:, c]) for c in cut], -1)
    rows = []
    for k, (r, i) in enumerate(parts):
        c, s = phase_ref[0, k : k + 1], phase_ref[1, k : k + 1]
        rows.append(jnp.concatenate([r * c - i * s, r * s + i * c], 1))
    z = product(jnp.concatenate(rows, 0), dft_ref, 0)
    rows = []
    for k in range(outer):
        r, i = z[lines * k : lines * (k + 1), :LANES], z[lines * k : lines * (k + 1), LANES:]
        c, s = phase_ref[2, k : k + 1], sign * phase_ref[3, k : k + 1]
        rows.append(jnp.concatenate([r * c - i * s, r * s + i * c], 1))
    z = product(jnp.concatenate(rows, 0), dft_ref, 2)
    parts = []
    for k in range(outer):
        r, i = z[lines * k : lines * (k + 1), :LANES], z[lines * k : lines * (k + 1), LANES:]
        c, s = phase_ref[0, k : k + 1], phase_ref[1, k : k + 1]
        parts.append((r * c + i * s, i * c - r * s))
    parts = small_dft(parts, 1)
    return jnp.concatenate([p[0] for p in parts], 1), jnp.concatenate([p[1] for p in parts], 1)


def cos_sin(x):
    y = x * x
    c = jnp.full_like(x, 1.0 / math.factorial(16))
    for n in range(14, -1, -2):
        c = c * -y + 1.0 / math.factorial(n)
    s = jnp.full_like(x, 1.0 / math.factorial(15))
    for n in range(13, 0, -2):
        s = s * -y + 1.0 / math.factorial(n)
    return c, s * x


def mega_kernel(
    depth_count,
    screens_ref, wave_ref, target_ref, dft_ref, phase_ref,
    out_ref,
    field, result, kept, angle, grads, send, recv,
    send_sem, recv_sem, out_sem, in_sem, back_out_sem, back_in_sem,
):
    _, lines, cells = wave_ref.shape
    count = cells // lines
    per_tile = max(1, LANES // lines)
    depth_at, trans_at = lax.axis_index("depth"), lax.axis_index("trans")
    me = trans_at * depth_count + depth_at
    step = min(16, lines)

    def device(at):
        return {"trans": at // depth_count, "depth": at % depth_count}

    def remote(slot, to, owner):
        return pltpu.make_async_remote_copy(
            src_ref=send.at[slot, to],
            dst_ref=recv.at[slot, owner],
            send_sem=send_sem.at[slot, to],
            recv_sem=recv_sem.at[slot, owner],
            device_id=device(to),
            device_id_type=pl.DeviceIdType.MESH,
        )

    def turn_start(slot, top, bottom):
        tiles = cells // LANES

        @pl.loop(0, tiles)
        def _(turn_at):
            tile = lax.rem(me * lines // LANES + turn_at, tiles)
            cols = pl.ds(pl.multiple_of(tile * LANES, LANES), LANES)
            block = jnp.concatenate([top[:, cols], bottom[:, cols]], 0).T
            for part in range(per_tile):
                to = tile * per_tile + part
                send[slot, to] = block[part * lines : (part + 1) * lines]

                @pl.when(to != me)
                def _():
                    remote(slot, to, me).start()

        recv[slot, me] = send[slot, me]

    def turn_wait(slot):
        @pl.loop(0, count)
        def _(at):
            @pl.when(at != me)
            def _():
                remote(slot, at, at).wait_recv()
                remote(slot, at, at).wait_send()

    def arrived(slot, here):
        blocks = [recv[slot, at, here] for at in range(count)]
        return (
            jnp.concatenate([b[:, :lines] for b in blocks], 1),
            jnp.concatenate([b[:, lines:] for b in blocks], 1),
        )

    def chunks(body):
        @pl.loop(0, lines // step)
        def _(at):
            body(pl.ds(pl.multiple_of(at * step, step), step))

    def screen_copy(to, owner):
        return pltpu.make_async_remote_copy(
            src_ref=screens_ref.at[0, pl.ds(to * lines, lines)],
            dst_ref=angle.at[owner],
            send_sem=out_sem.at[to],
            recv_sem=in_sem.at[owner],
            device_id={"depth": to, "trans": trans_at},
            device_id_type=pl.DeviceIdType.MESH,
        )

    def grad_copy(to, owner):
        return pltpu.make_async_remote_copy(
            src_ref=grads.at[to],
            dst_ref=out_ref.at[0, pl.ds(pl.multiple_of(owner * lines, lines), lines)],
            send_sem=back_out_sem.at[to],
            recv_sem=back_in_sem.at[owner],
            device_id={"depth": to, "trans": trans_at},
            device_id_type=pl.DeviceIdType.MESH,
        )

    def grad_start(to):
        @pl.when(depth_at != to)
        def _():
            grad_copy(to, depth_at).start()

        @pl.when(depth_at == to)
        def _():
            out_ref[0, pl.ds(to * lines, lines)] = grads[to]

    barrier = pltpu.get_barrier_semaphore()

    @pl.loop(0, count)
    def _(at):
        @pl.when(at != me)
        def _():
            pl.semaphore_signal(
                barrier, inc=1, device_id=device(at), device_id_type=pl.DeviceIdType.MESH
            )

    pl.semaphore_wait(barrier, count - 1)

    for to in range(depth_count):
        @pl.when(depth_at != to)
        def _():
            screen_copy(to, depth_at).start()

        @pl.when(depth_at == to)
        def _():
            angle[to] = screens_ref[0, pl.ds(to * lines, lines)]

    def start_field(here):
        field[0, here] = wave_ref[0, here]
        field[1, here] = wave_ref[1, here]

    chunks(start_field)
    for to in range(depth_count):
        @pl.when(depth_at != to)
        def _():
            screen_copy(to, to).wait_recv()
            screen_copy(to, to).wait_send()

    turn_start(2, angle.at[1], angle.at[3])

    @pl.loop(0, depth_count)
    def _(g):
        @pl.when(g == 1)
        def _():
            turn_wait(2)

            def unpack(here):
                angle[1, here], angle[3, here] = arrived(2, here)

            chunks(unpack)

        def before(here):
            c, s = cos_sin(angle[g, here])
            r, i = field[0, here], field[1, here]
            r, i = r * c - i * s, r * s + i * c
            kept[g, 0, here] = r
            kept[g, 1, here] = i
            result[0, here], result[1, here] = chunk_pass(r, i, dft_ref, phase_ref, 1.0)

        def after(here):
            r, i = arrived(g % 2, here)
            field[0, here], field[1, here] = chunk_pass(r, i, dft_ref, phase_ref, 1.0)

        chunks(before)
        turn_start(g % 2, result.at[0], result.at[1])
        turn_wait(g % 2)
        chunks(after)

    def residual(here):
        field[0, here] = field[0, here] - target_ref[0, here]
        field[1, here] = field[1, here] - target_ref[1, here]

    chunks(residual)

    @pl.loop(0, depth_count)
    def _(at):
        g = depth_count - 1 - at

        def before(here):
            result[0, here], result[1, here] = chunk_pass(
                field[0, here], field[1, here], dft_ref, phase_ref, -1.0
            )

        def after(here):
            r, i = arrived(at % 2, here)
            r, i = chunk_pass(r, i, dft_ref, phase_ref, -1.0)
            grads[g, here] = i * kept[g, 0, here] - r * kept[g, 1, here]
            c, s = cos_sin(angle[g, here])
            field[0, here] = r * c + i * s
            field[1, here] = i * c - r * s

        chunks(before)
        turn_start(at % 2, result.at[0], result.at[1])
        turn_wait(at % 2)
        chunks(after)

        @pl.when(g == 2)
        def _():
            grad_start(2)

        @pl.when(g == 1)
        def _():
            turn_start(3, grads.at[1], grads.at[3])

    grad_start(0)
    turn_wait(3)

    def unpack(here):
        grads[1, here], grads[3, here] = arrived(3, here)

    chunks(unpack)
    grad_start(1)
    grad_start(3)
    for to in range(depth_count):
        @pl.when(depth_at != to)
        def _():
            grad_copy(to, to).wait_recv()
            grad_copy(to, to).wait_send()


def whole_chain(screens, wave, target, tables, depth_count):
    two, lines, cells = wave.shape
    count = cells // lines
    f32 = jnp.float32
    whole = pl.BlockSpec(memory_space=pltpu.VMEM)
    return pl.pallas_call(
        functools.partial(mega_kernel, depth_count),
        out_shape=jax.ShapeDtypeStruct(screens.shape, f32),
        in_specs=[whole] * 5,
        out_specs=whole,
        scratch_shapes=[
            pltpu.VMEM((two, lines, cells), f32),
            pltpu.VMEM((two, lines, cells), f32),
            pltpu.VMEM((depth_count, two, lines, cells), f32),
            pltpu.VMEM((depth_count, lines, cells), f32),
            pltpu.VMEM((depth_count, lines, cells), f32),
            pltpu.VMEM((4, count, lines, two * lines), f32),
            pltpu.VMEM((4, count, lines, two * lines), f32),
            pltpu.SemaphoreType.DMA((4, count)),
            pltpu.SemaphoreType.DMA((4, count)),
            pltpu.SemaphoreType.DMA((depth_count,)),
            pltpu.SemaphoreType.DMA((depth_count,)),
            pltpu.SemaphoreType.DMA((depth_count,)),
            pltpu.SemaphoreType.DMA((depth_count,)),
        ],
        compiler_params=pltpu.CompilerParams(
            collective_id=0, has_side_effects=True, vmem_limit_bytes=56 << 20
        ),
        name="whole_chain",
    )(screens, wave, target, *tables)


def illumination(angle_index, first, lines, cells):
    def wave(positions, tilt):
        turns = lax.rem(lax.rem(positions * tilt, cells) + cells, cells)
        radians = TWO_PI / cells * turns.astype(jnp.float32)
        return jnp.cos(radians), jnp.sin(radians)

    column = wave(jnp.arange(cells, dtype=jnp.int32), angle_index[0, 0])
    row = wave(first + jnp.arange(lines, dtype=jnp.int32), angle_index[0, 1])
    cc, cs = column[0][None], column[1][None]
    rc, rs = row[0][:, None], row[1][:, None]
    return jnp.stack((cc * rc - cs * rs, cc * rs + cs * rc))


def on_device(screens, measured, angle_index):
    depth_count = lax.axis_size("depth")
    held, cells = screens.shape[1:]
    lines = held // depth_count
    depth_at = lax.axis_index("depth")
    first = lax.axis_index("trans") * held + depth_at * lines
    tables = [jnp.asarray(t) for t in tables_of(cells)]

    wave = illumination(angle_index, first, lines, cells)
    target = lax.dynamic_slice_in_dim(measured[0], depth_at * lines, lines, 1)
    return whole_chain(screens, wave, target.astype(jnp.float32), tables, depth_count)


def solution(mesh):
    placed = (P("depth", "trans", None), P(None, None, "trans", None), P())
    return jax.shard_map(
        on_device, mesh=mesh, in_specs=placed, out_specs=P("depth", "trans", None), check_vma=False
    )
```

```python
import functools
import math

import jax
import jax.numpy as jnp
import numpy as np
from jax import lax
from jax.experimental import pallas as pl
from jax.experimental.pallas import tpu as pltpu
from jax.sharding import PartitionSpec as P

TWO_PI = 2.0 * math.pi
LANES = 128


def as_pair(table):
    high = np.asarray(table, np.float32).astype(jnp.bfloat16)
    low = (np.asarray(table, np.float64) - high.astype(np.float64)).astype(jnp.bfloat16)
    return high, low


def tables_of(cells):
    outer = cells // LANES
    at = np.arange(LANES)
    radians = -TWO_PI / LANES * (at[:, None] * at[None, :] % LANES)
    c, s = np.cos(radians), np.sin(radians)
    ahead = np.block([[c, s], [-s, c]])
    back = np.block([[c, -s], [s, c]])
    k = np.arange(outer)[:, None]
    twist = -TWO_PI / cells * (k * at[None, :] % cells)
    freq = k + outer * at[None, :]
    signed = np.where(freq < cells // 2, freq, freq - cells)
    spread = -TWO_PI / (8 * cells) * (signed * signed % (8 * cells))
    phases = np.stack(
        [np.cos(twist), np.sin(twist), np.cos(spread) / cells, np.sin(spread) / cells]
    ).astype(np.float32)
    dft = np.stack([*as_pair(ahead), *as_pair(back)])
    return dft, phases


def small_dft(parts, sign):
    count = len(parts)
    if count == 1:
        return parts
    even = small_dft(parts[0::2], sign)
    odd = small_dft(parts[1::2], sign)
    low, high = [], []
    for k in range(count // 2):
        (er, ei), (r, i) = even[k], odd[k]
        turn = 8 * k / count
        if turn == 2:
            r, i = (-i, r) if sign > 0 else (i, -r)
        elif turn == 1:
            h = math.sqrt(0.5)
            r, i = (h * (r - sign * i), h * (i + sign * r))
        elif turn == 3:
            h = math.sqrt(0.5)
            r, i = (-h * (r + sign * i), h * (sign * r - i))
        elif k:
            c, s = math.cos(TWO_PI * k / count), sign * math.sin(TWO_PI * k / count)
            r, i = (r * c - i * s, r * s + i * c)
        low.append((er + r, ei + i))
        high.append((er - r, ei - i))
    return low + high


def product(value, dft_ref, high):
    top = value.astype(jnp.bfloat16)
    rest = (value - top.astype(jnp.float32)).astype(jnp.bfloat16)
    dot = functools.partial(jnp.dot, preferred_element_type=jnp.float32)
    return dot(top, dft_ref[high]) + (dot(top, dft_ref[high + 1]) + dot(rest, dft_ref[high]))


def chunk_pass(re, im, dft_ref, phase_ref, sign):
    lines, cells = re.shape
    outer = cells // LANES
    cut = [slice(LANES * a, LANES * (a + 1)) for a in range(outer)]
    parts = small_dft([(re[:, c], im[:, c]) for c in cut], -1)
    rows = []
    for k, (r, i) in enumerate(parts):
        c, s = phase_ref[0, k : k + 1], phase_ref[1, k : k + 1]
        rows.append(jnp.concatenate([r * c - i * s, r * s + i * c], 1))
    z = product(jnp.concatenate(rows, 0), dft_ref, 0)
    rows = []
    for k in range(outer):
        r, i = z[lines * k : lines * (k + 1), :LANES], z[lines * k : lines * (k + 1), LANES:]
        c, s = phase_ref[2, k : k + 1], sign * phase_ref[3, k : k + 1]
        rows.append(jnp.concatenate([r * c - i * s, r * s + i * c], 1))
    z = product(jnp.concatenate(rows, 0), dft_ref, 2)
    parts = []
    for k in range(outer):
        r, i = z[lines * k : lines * (k + 1), :LANES], z[lines * k : lines * (k + 1), LANES:]
        c, s = phase_ref[0, k : k + 1], phase_ref[1, k : k + 1]
        parts.append((r * c + i * s, i * c - r * s))
    parts = small_dft(parts, 1)
    return jnp.concatenate([p[0] for p in parts], 1), jnp.concatenate([p[1] for p in parts], 1)


def cos_sin(x):
    y = x * x
    c = jnp.full_like(x, 1.0 / math.factorial(16))
    for n in range(14, -1, -2):
        c = c * -y + 1.0 / math.factorial(n)
    s = jnp.full_like(x, 1.0 / math.factorial(15))
    for n in range(13, 0, -2):
        s = s * -y + 1.0 / math.factorial(n)
    return c, s * x


def mega_kernel(
    depth_count,
    screens_ref, wave_ref, target_ref, dft_ref, phase_ref,
    out_ref,
    result, kept, angle, grads, send, recv,
    send_sem, recv_sem, out_sem, in_sem, back_out_sem, back_in_sem,
):
    _, lines, cells = wave_ref.shape
    count = cells // lines
    per_tile = max(1, LANES // lines)
    depth_at, trans_at = lax.axis_index("depth"), lax.axis_index("trans")
    me = trans_at * depth_count + depth_at
    step = min(16, lines)
    stages = lines // step

    def device(at):
        return {"trans": at // depth_count, "depth": at % depth_count}

    def remote(slot, stage, to):
        return pltpu.make_async_remote_copy(
            src_ref=send.at[slot, stage, to],
            dst_ref=recv.at[slot, stage, me],
            send_sem=send_sem.at[slot],
            recv_sem=recv_sem.at[slot, stage],
            device_id=device(to),
            device_id_type=pl.DeviceIdType.MESH,
        )

    def send_to(slot, stage, to):
        @pl.when(to != me)
        def _():
            remote(slot, stage, to).start()

    def turn_start(slot, top, bottom):
        tiles = cells // LANES

        @pl.loop(0, tiles)
        def _(turn_at):
            tile = lax.rem(me * lines // LANES + turn_at, tiles)
            cols = pl.ds(pl.multiple_of(tile * LANES, LANES), LANES)
            block = jnp.concatenate([top[:, cols], bottom[:, cols]], 0).T
            for part in range(per_tile):
                to = tile * per_tile + part
                for stage in range(stages):
                    begin = part * lines + stage * step
                    send[slot, stage, to] = block[begin : begin + step]
                send_to(slot, 0, to)

        for stage in range(stages):
            recv[slot, stage, me] = send[slot, stage, me]

        @pl.loop(count, stages * count)
        def _(at):
            send_to(slot, at // count, lax.rem(me + at, count))

    def wait_stage(slot, stage):
        part = recv.at[slot, stage, pl.ds(0, count - 1)]
        pltpu.make_async_copy(part, part, recv_sem.at[slot, stage]).wait()

    def wait_sent(slot):
        for stage in range(stages):
            part = send.at[slot, stage, pl.ds(0, count - 1)]
            pltpu.make_async_copy(part, part, send_sem.at[slot]).wait()

    def arrived(slot, stage):
        blocks = [recv[slot, stage, at] for at in range(count)]
        return (
            jnp.concatenate([b[:, :lines] for b in blocks], 1),
            jnp.concatenate([b[:, lines:] for b in blocks], 1),
        )

    def chunks(body):
        @pl.loop(0, stages)
        def _(at):
            body(at, pl.ds(pl.multiple_of(at * step, step), step))

    def line_chunk(re, im, sign):
        return chunk_pass(re, im, dft_ref, phase_ref, sign)

    def screen_copy(to, owner):
        return pltpu.make_async_remote_copy(
            src_ref=screens_ref.at[0, pl.ds(to * lines, lines)],
            dst_ref=angle.at[owner],
            send_sem=out_sem.at[to],
            recv_sem=in_sem.at[owner],
            device_id={"depth": to, "trans": trans_at},
            device_id_type=pl.DeviceIdType.MESH,
        )

    def grad_copy(to, owner, begin, size):
        rows = pl.ds(pl.multiple_of(owner * lines + begin, size), size)
        return pltpu.make_async_remote_copy(
            src_ref=grads.at[to, pl.ds(begin, size)],
            dst_ref=out_ref.at[0, rows],
            send_sem=back_out_sem.at[to],
            recv_sem=back_in_sem.at[owner],
            device_id={"depth": to, "trans": trans_at},
            device_id_type=pl.DeviceIdType.MESH,
        )

    def grad_start(to, at):
        begin = pl.multiple_of(at * step, step)

        @pl.when(depth_at != to)
        def _():
            grad_copy(to, depth_at, begin, step).start()

        @pl.when(depth_at == to)
        def _():
            out_ref[0, pl.ds(to * lines + begin, step)] = grads[to, pl.ds(begin, step)]

    barrier = pltpu.get_barrier_semaphore()

    @pl.loop(0, count)
    def _(at):
        @pl.when(at != me)
        def _():
            pl.semaphore_signal(
                barrier, inc=1, device_id=device(at), device_id_type=pl.DeviceIdType.MESH
            )

    pl.semaphore_wait(barrier, count - 1)

    for to in range(depth_count):
        @pl.when(depth_at != to)
        def _():
            screen_copy(to, depth_at).start()

        @pl.when(depth_at == to)
        def _():
            angle[to] = screens_ref[0, pl.ds(to * lines, lines)]

    for to in range(depth_count):
        @pl.when(depth_at != to)
        def _():
            screen_copy(to, to).wait_recv()
            screen_copy(to, to).wait_send()

    turn_start(2, angle.at[1], angle.at[3])

    def enter(g, r, i, here):
        c, s = cos_sin(angle[g, here])
        r, i = r * c - i * s, r * s + i * c
        kept[g, 0, here] = r
        kept[g, 1, here] = i
        result[0, here], result[1, here] = line_chunk(r, i, 1.0)

    def leave(g, r, i, here):
        grads[g, here] = i * kept[g, 0, here] - r * kept[g, 1, here]

    def first(at, here):
        enter(0, wave_ref[0, here], wave_ref[1, here], here)

    chunks(first)
    turn_start(0, result.at[0], result.at[1])

    def unpack_screens(at, here):
        wait_stage(2, at)
        angle[1, here], angle[3, here] = arrived(2, at)

    chunks(unpack_screens)
    wait_sent(2)

    @pl.loop(1, depth_count)
    def _(g):
        slot = (g - 1) % 2

        def body(at, here):
            wait_stage(slot, at)
            r, i = line_chunk(*arrived(slot, at), 1.0)
            enter(g, r, i, here)

        chunks(body)
        wait_sent(slot)
        turn_start(g % 2, result.at[0], result.at[1])

    last = (depth_count - 1) % 2

    def residual(at, here):
        wait_stage(last, at)
        r, i = line_chunk(*arrived(last, at), 1.0)
        r, i = r - target_ref[0, here], i - target_ref[1, here]
        result[0, here], result[1, here] = line_chunk(r, i, -1.0)

    chunks(residual)
    wait_sent(last)
    turn_start(1 - last, result.at[0], result.at[1])

    @pl.loop(1, depth_count)
    def _(turned):
        g = depth_count - turned
        slot = (last + turned) % 2

        def body(at, here):
            wait_stage(slot, at)
            r, i = line_chunk(*arrived(slot, at), -1.0)
            leave(g, r, i, here)
            c, s = cos_sin(angle[g, here])
            r, i = r * c + i * s, i * c - r * s
            result[0, here], result[1, here] = line_chunk(r, i, -1.0)

            @pl.when(g == 2)
            def _():
                grad_start(2, at)

        chunks(body)
        wait_sent(slot)

        @pl.when(g == 1)
        def _():
            turn_start(3, grads.at[1], grads.at[3])

        turn_start(1 - slot, result.at[0], result.at[1])

    def unpack_grads(at, here):
        wait_stage(3, at)
        grads[1, here], grads[3, here] = arrived(3, at)
        grad_start(1, at)
        grad_start(3, at)

    chunks(unpack_grads)
    wait_sent(3)
    slot = (last + depth_count) % 2

    def final(at, here):
        wait_stage(slot, at)
        r, i = line_chunk(*arrived(slot, at), -1.0)
        leave(0, r, i, here)
        grad_start(0, at)

    chunks(final)
    wait_sent(slot)
    for to in range(depth_count):
        @pl.when(depth_at != to)
        def _():
            grad_copy(to, to, 0, lines).wait_recv()
            grad_copy(to, to, 0, lines).wait_send()


def whole_chain(screens, wave, target, tables, depth_count):
    two, lines, cells = wave.shape
    count = cells // lines
    step = min(16, lines)
    stages = lines // step
    f32 = jnp.float32
    whole = pl.BlockSpec(memory_space=pltpu.VMEM)
    return pl.pallas_call(
        functools.partial(mega_kernel, depth_count),
        out_shape=jax.ShapeDtypeStruct(screens.shape, f32),
        in_specs=[whole] * 5,
        out_specs=whole,
        scratch_shapes=[
            pltpu.VMEM((two, lines, cells), f32),
            pltpu.VMEM((depth_count, two, lines, cells), f32),
            pltpu.VMEM((depth_count, lines, cells), f32),
            pltpu.VMEM((depth_count, lines, cells), f32),
            pltpu.VMEM((4, stages, count, step, two * lines), f32),
            pltpu.VMEM((4, stages, count, step, two * lines), f32),
            pltpu.SemaphoreType.DMA((4,)),
            pltpu.SemaphoreType.DMA((4, stages)),
            pltpu.SemaphoreType.DMA((depth_count,)),
            pltpu.SemaphoreType.DMA((depth_count,)),
            pltpu.SemaphoreType.DMA((depth_count,)),
            pltpu.SemaphoreType.DMA((depth_count,)),
        ],
        compiler_params=pltpu.CompilerParams(
            collective_id=0, has_side_effects=True, vmem_limit_bytes=56 << 20
        ),
        name="whole_chain",
    )(screens, wave, target, *tables)


def illumination(angle_index, first, lines, cells):
    def wave(positions, tilt):
        turns = lax.rem(lax.rem(positions * tilt, cells) + cells, cells)
        radians = TWO_PI / cells * turns.astype(jnp.float32)
        return jnp.cos(radians), jnp.sin(radians)

    column = wave(jnp.arange(cells, dtype=jnp.int32), angle_index[0, 0])
    row = wave(first + jnp.arange(lines, dtype=jnp.int32), angle_index[0, 1])
    cc, cs = column[0][None], column[1][None]
    rc, rs = row[0][:, None], row[1][:, None]
    return jnp.stack((cc * rc - cs * rs, cc * rs + cs * rc))


def on_device(screens, measured, angle_index):
    depth_count = lax.axis_size("depth")
    held, cells = screens.shape[1:]
    lines = held // depth_count
    depth_at = lax.axis_index("depth")
    first = lax.axis_index("trans") * held + depth_at * lines
    tables = [jnp.asarray(t) for t in tables_of(cells)]

    wave = illumination(angle_index, first, lines, cells)
    target = lax.dynamic_slice_in_dim(measured[0], depth_at * lines, lines, 1)
    return whole_chain(screens, wave, target.astype(jnp.float32), tables, depth_count)


def solution(mesh):
    placed = (P("depth", "trans", None), P(None, None, "trans", None), P())
    return jax.shard_map(
        on_device, mesh=mesh, in_specs=placed, out_specs=P("depth", "trans", None), check_vma=False
    )
```

```python
import functools
import math

import jax
import jax.numpy as jnp
import numpy as np
from jax import lax
from jax.experimental import pallas as pl
from jax.experimental.pallas import tpu as pltpu
from jax.sharding import PartitionSpec as P

TWO_PI = 2.0 * math.pi
LANES = 128


def as_pair(table):
    high = np.asarray(table, np.float32).astype(jnp.bfloat16)
    low = (np.asarray(table, np.float64) - high.astype(np.float64)).astype(jnp.bfloat16)
    return high, low


def tables_of(cells):
    outer = cells // LANES
    at = np.arange(LANES)
    radians = -TWO_PI / LANES * (at[:, None] * at[None, :] % LANES)
    c, s = np.cos(radians), np.sin(radians)
    ahead = np.block([[c, s], [-s, c]])
    back = np.block([[c, -s], [s, c]])
    k = np.arange(outer)[:, None]
    twist = -TWO_PI / cells * (k * at[None, :] % cells)
    freq = k + outer * at[None, :]
    signed = np.where(freq < cells // 2, freq, freq - cells)
    spread = -TWO_PI / (8 * cells) * (signed * signed % (8 * cells))
    phases = np.stack(
        [np.cos(twist), np.sin(twist), np.cos(spread) / cells, np.sin(spread) / cells]
    ).astype(np.float32)
    dft = np.stack([*as_pair(ahead), *as_pair(back)])
    return dft, phases


def small_dft(parts, sign):
    count = len(parts)
    if count == 1:
        return parts
    even = small_dft(parts[0::2], sign)
    odd = small_dft(parts[1::2], sign)
    low, high = [], []
    for k in range(count // 2):
        (er, ei), (r, i) = even[k], odd[k]
        turn = 8 * k / count
        if turn == 2:
            r, i = (-i, r) if sign > 0 else (i, -r)
        elif turn == 1:
            h = math.sqrt(0.5)
            r, i = (h * (r - sign * i), h * (i + sign * r))
        elif turn == 3:
            h = math.sqrt(0.5)
            r, i = (-h * (r + sign * i), h * (sign * r - i))
        elif k:
            c, s = math.cos(TWO_PI * k / count), sign * math.sin(TWO_PI * k / count)
            r, i = (r * c - i * s, r * s + i * c)
        low.append((er + r, ei + i))
        high.append((er - r, ei - i))
    return low + high


def product(value, dft_ref, high):
    top = value.astype(jnp.bfloat16)
    rest = (value - top.astype(jnp.float32)).astype(jnp.bfloat16)
    dot = functools.partial(jnp.dot, preferred_element_type=jnp.float32)
    return dot(top, dft_ref[high]) + (dot(top, dft_ref[high + 1]) + dot(rest, dft_ref[high]))


def chunk_pass(re, im, dft_ref, phase_ref, sign):
    lines, cells = re.shape
    outer = cells // LANES
    cut = [slice(LANES * a, LANES * (a + 1)) for a in range(outer)]
    parts = small_dft([(re[:, c], im[:, c]) for c in cut], -1)
    rows = []
    for k, (r, i) in enumerate(parts):
        c, s = phase_ref[0, k : k + 1], phase_ref[1, k : k + 1]
        rows.append(jnp.concatenate([r * c - i * s, r * s + i * c], 1))
    z = product(jnp.concatenate(rows, 0), dft_ref, 0)
    rows = []
    for k in range(outer):
        r, i = z[lines * k : lines * (k + 1), :LANES], z[lines * k : lines * (k + 1), LANES:]
        c, s = phase_ref[2, k : k + 1], sign * phase_ref[3, k : k + 1]
        rows.append(jnp.concatenate([r * c - i * s, r * s + i * c], 1))
    z = product(jnp.concatenate(rows, 0), dft_ref, 2)
    parts = []
    for k in range(outer):
        r, i = z[lines * k : lines * (k + 1), :LANES], z[lines * k : lines * (k + 1), LANES:]
        c, s = phase_ref[0, k : k + 1], phase_ref[1, k : k + 1]
        parts.append((r * c + i * s, i * c - r * s))
    parts = small_dft(parts, 1)
    return jnp.concatenate([p[0] for p in parts], 1), jnp.concatenate([p[1] for p in parts], 1)


def cos_sin(x):
    y = x * x
    c = jnp.full_like(x, 1.0 / math.factorial(16))
    for n in range(14, -1, -2):
        c = c * -y + 1.0 / math.factorial(n)
    s = jnp.full_like(x, 1.0 / math.factorial(15))
    for n in range(13, 0, -2):
        s = s * -y + 1.0 / math.factorial(n)
    return c, s * x


def mega_kernel(
    depth_count,
    screens_ref, wave_ref, target_ref, dft_ref, phase_ref,
    out_ref,
    result, kept, angle, grads, send, recv,
    send_sem, recv_sem, out_sem, in_sem, back_out_sem, back_in_sem,
):
    _, lines, cells = wave_ref.shape
    count = cells // lines
    per_tile = max(1, LANES // lines)
    depth_at, trans_at = lax.axis_index("depth"), lax.axis_index("trans")
    me = trans_at * depth_count + depth_at
    step = min(16, lines)
    stages = lines // step

    def device(at):
        return {"trans": at // depth_count, "depth": at % depth_count}

    def remote(slot, stage, to):
        return pltpu.make_async_remote_copy(
            src_ref=send.at[slot, stage, to],
            dst_ref=recv.at[slot, stage, me],
            send_sem=send_sem.at[slot],
            recv_sem=recv_sem.at[slot, stage],
            device_id=device(to),
            device_id_type=pl.DeviceIdType.MESH,
        )

    def send_to(slot, stage, to):
        @pl.when(to != me)
        def _():
            remote(slot, stage, to).start()

    def turn_start(slot, top, bottom):
        tiles = cells // LANES

        @pl.loop(0, tiles, unroll=2)
        def _(turn_at):
            tile = lax.rem(me * lines // LANES + turn_at, tiles)
            cols = pl.ds(pl.multiple_of(tile * LANES, LANES), LANES)
            block = jnp.concatenate([top[:, cols], bottom[:, cols]], 0).T
            for part in range(per_tile):
                to = tile * per_tile + part
                for stage in range(stages):
                    begin = part * lines + stage * step
                    send[slot, stage, to] = block[begin : begin + step]
                send_to(slot, 0, to)

        for stage in range(stages):
            recv[slot, stage, me] = send[slot, stage, me]

        @pl.loop(count, stages * count)
        def _(at):
            send_to(slot, at // count, lax.rem(me + at, count))

    def wait_stage(slot, stage):
        part = recv.at[slot, stage, pl.ds(0, count - 1)]
        pltpu.make_async_copy(part, part, recv_sem.at[slot, stage]).wait()

    def wait_sent(slot):
        for stage in range(stages):
            part = send.at[slot, stage, pl.ds(0, count - 1)]
            pltpu.make_async_copy(part, part, send_sem.at[slot]).wait()

    def arrived(slot, stage):
        blocks = [recv[slot, stage, at] for at in range(count)]
        return (
            jnp.concatenate([b[:, :lines] for b in blocks], 1),
            jnp.concatenate([b[:, lines:] for b in blocks], 1),
        )

    def chunks(body, unroll=False):
        @pl.loop(0, stages, unroll=unroll)
        def _(at):
            body(at, pl.ds(pl.multiple_of(at * step, step), step))

    def line_chunk(re, im, sign):
        return chunk_pass(re, im, dft_ref, phase_ref, sign)

    def screen_copy(to, owner):
        return pltpu.make_async_remote_copy(
            src_ref=screens_ref.at[0, pl.ds(to * lines, lines)],
            dst_ref=angle.at[owner],
            send_sem=out_sem.at[to],
            recv_sem=in_sem.at[owner],
            device_id={"depth": to, "trans": trans_at},
            device_id_type=pl.DeviceIdType.MESH,
        )

    def grad_copy(to, owner, begin, size):
        rows = pl.ds(pl.multiple_of(owner * lines + begin, size), size)
        return pltpu.make_async_remote_copy(
            src_ref=grads.at[to, pl.ds(begin, size)],
            dst_ref=out_ref.at[0, rows],
            send_sem=back_out_sem.at[to],
            recv_sem=back_in_sem.at[owner],
            device_id={"depth": to, "trans": trans_at},
            device_id_type=pl.DeviceIdType.MESH,
        )

    def grad_start(to, at):
        begin = pl.multiple_of(at * step, step)

        @pl.when(depth_at != to)
        def _():
            grad_copy(to, depth_at, begin, step).start()

        @pl.when(depth_at == to)
        def _():
            out_ref[0, pl.ds(to * lines + begin, step)] = grads[to, pl.ds(begin, step)]

    barrier = pltpu.get_barrier_semaphore()

    @pl.loop(0, count)
    def _(at):
        @pl.when(at != me)
        def _():
            pl.semaphore_signal(
                barrier, inc=1, device_id=device(at), device_id_type=pl.DeviceIdType.MESH
            )

    pl.semaphore_wait(barrier, count - 1)

    def share_screen():
        for to in range(depth_count):
            @pl.when(depth_at != to)
            def _():
                screen_copy(to, depth_at).start()

            @pl.when(depth_at == to)
            def _():
                angle[to] = screens_ref[0, pl.ds(to * lines, lines)]

    @pl.when(depth_at == 0)
    def _():
        share_screen()

    @pl.when(depth_at != 0)
    def _():
        screen_copy(0, 0).wait_recv()

    def enter(g, r, i, here):
        c, s = cos_sin(angle[g, here])
        r, i = r * c - i * s, r * s + i * c
        kept[g, 0, here] = r
        kept[g, 1, here] = i
        result[0, here], result[1, here] = line_chunk(r, i, 1.0)

    def leave(g, r, i, here):
        grads[g, here] = i * kept[g, 0, here] - r * kept[g, 1, here]

    def first(at, here):
        enter(0, wave_ref[0, here], wave_ref[1, here], here)

    chunks(first, True)
    turn_start(0, result.at[0], result.at[1])

    @pl.when(depth_at != 0)
    def _():
        share_screen()

    for to in range(depth_count):
        @pl.when(depth_at != to)
        def _():
            if to:
                screen_copy(to, to).wait_recv()
            screen_copy(to, to).wait_send()

    turn_start(2, angle.at[1], angle.at[3])

    @pl.loop(1, depth_count)
    def _(g):
        slot = (g - 1) % 2

        def body(at, here):
            wait_stage(slot, at)
            r, i = line_chunk(*arrived(slot, at), 1.0)

            @pl.when(g == 1)
            def _():
                wait_stage(2, at)
                angle[1, here], angle[3, here] = arrived(2, at)

            enter(g, r, i, here)

        chunks(body)
        wait_sent(slot)

        @pl.when(g == 1)
        def _():
            wait_sent(2)

        turn_start(g % 2, result.at[0], result.at[1])

    last = (depth_count - 1) % 2

    def residual(at, here):
        wait_stage(last, at)
        r, i = line_chunk(*arrived(last, at), 1.0)
        r, i = r - target_ref[0, here], i - target_ref[1, here]
        result[0, here], result[1, here] = line_chunk(r, i, -1.0)

    chunks(residual)
    wait_sent(last)
    turn_start(1 - last, result.at[0], result.at[1])

    @pl.loop(1, depth_count)
    def _(turned):
        g = depth_count - turned
        slot = (last + turned) % 2

        def body(at, here):
            wait_stage(slot, at)
            r, i = line_chunk(*arrived(slot, at), -1.0)
            leave(g, r, i, here)
            c, s = cos_sin(angle[g, here])
            r, i = r * c + i * s, i * c - r * s
            result[0, here], result[1, here] = line_chunk(r, i, -1.0)

            @pl.when(g == 2)
            def _():
                grad_start(2, at)

        chunks(body)
        wait_sent(slot)

        @pl.when(g == 1)
        def _():
            turn_start(3, grads.at[1], grads.at[3])

        turn_start(1 - slot, result.at[0], result.at[1])

    def unpack_grads(at, here):
        wait_stage(3, at)
        grads[1, here], grads[3, here] = arrived(3, at)
        grad_start(1, at)
        grad_start(3, at)

    chunks(unpack_grads)
    wait_sent(3)
    slot = (last + depth_count) % 2

    def final(at, here):
        wait_stage(slot, at)
        r, i = line_chunk(*arrived(slot, at), -1.0)
        leave(0, r, i, here)
        grad_start(0, at)

    chunks(final)
    wait_sent(slot)
    for to in range(depth_count):
        @pl.when(depth_at != to)
        def _():
            grad_copy(to, to, 0, lines).wait_recv()
            grad_copy(to, to, 0, lines).wait_send()


def whole_chain(screens, wave, target, tables, depth_count):
    two, lines, cells = wave.shape
    count = cells // lines
    step = min(16, lines)
    stages = lines // step
    f32 = jnp.float32
    whole = pl.BlockSpec(memory_space=pltpu.VMEM)
    return pl.pallas_call(
        functools.partial(mega_kernel, depth_count),
        out_shape=jax.ShapeDtypeStruct(screens.shape, f32),
        in_specs=[whole] * 5,
        out_specs=whole,
        scratch_shapes=[
            pltpu.VMEM((two, lines, cells), f32),
            pltpu.VMEM((depth_count, two, lines, cells), f32),
            pltpu.VMEM((depth_count, lines, cells), f32),
            pltpu.VMEM((depth_count, lines, cells), f32),
            pltpu.VMEM((4, stages, count, step, two * lines), f32),
            pltpu.VMEM((4, stages, count, step, two * lines), f32),
            pltpu.SemaphoreType.DMA((4,)),
            pltpu.SemaphoreType.DMA((4, stages)),
            pltpu.SemaphoreType.DMA((depth_count,)),
            pltpu.SemaphoreType.DMA((depth_count,)),
            pltpu.SemaphoreType.DMA((depth_count,)),
            pltpu.SemaphoreType.DMA((depth_count,)),
        ],
        compiler_params=pltpu.CompilerParams(
            collective_id=0, has_side_effects=True, vmem_limit_bytes=56 << 20
        ),
        name="whole_chain",
    )(screens, wave, target, *tables)


def illumination(angle_index, first, lines, cells):
    def wave(positions, tilt):
        turns = lax.rem(lax.rem(positions * tilt, cells) + cells, cells)
        radians = TWO_PI / cells * turns.astype(jnp.float32)
        return jnp.cos(radians), jnp.sin(radians)

    column = wave(jnp.arange(cells, dtype=jnp.int32), angle_index[0, 0])
    row = wave(first + jnp.arange(lines, dtype=jnp.int32), angle_index[0, 1])
    cc, cs = column[0][None], column[1][None]
    rc, rs = row[0][:, None], row[1][:, None]
    return jnp.stack((cc * rc - cs * rs, cc * rs + cs * rc))


def on_device(screens, measured, angle_index):
    depth_count = lax.axis_size("depth")
    held, cells = screens.shape[1:]
    lines = held // depth_count
    depth_at = lax.axis_index("depth")
    first = lax.axis_index("trans") * held + depth_at * lines
    tables = [jnp.asarray(t) for t in tables_of(cells)]

    wave = illumination(angle_index, first, lines, cells)
    target = lax.dynamic_slice_in_dim(measured[0], depth_at * lines, lines, 1)
    return whole_chain(screens, wave, target.astype(jnp.float32), tables, depth_count)


def solution(mesh):
    placed = (P("depth", "trans", None), P(None, None, "trans", None), P())
    return jax.shard_map(
        on_device, mesh=mesh, in_specs=placed, out_specs=P("depth", "trans", None), check_vma=False
    )
```

```python
import functools
import math

import jax
import jax.numpy as jnp
import numpy as np
from jax import lax
from jax.experimental import pallas as pl
from jax.experimental.pallas import tpu as pltpu
from jax.sharding import PartitionSpec as P

TWO_PI = 2.0 * math.pi
LANES = 128


def as_pair(table):
    high = np.asarray(table, np.float32).astype(jnp.bfloat16)
    low = (np.asarray(table, np.float64) - high.astype(np.float64)).astype(jnp.bfloat16)
    return high, low


def tables_of(cells):
    outer = cells // LANES
    at = np.arange(LANES)
    radians = -TWO_PI / LANES * (at[:, None] * at[None, :] % LANES)
    c, s = np.cos(radians), np.sin(radians)
    ahead = np.block([[c, s], [-s, c]])
    back = np.block([[c, -s], [s, c]])
    k = np.arange(outer)[:, None]
    twist = -TWO_PI / cells * (k * at[None, :] % cells)
    freq = k + outer * at[None, :]
    signed = np.where(freq < cells // 2, freq, freq - cells)
    spread = -TWO_PI / (8 * cells) * (signed * signed % (8 * cells))
    phases = np.stack(
        [np.cos(twist), np.sin(twist), np.cos(spread) / cells, np.sin(spread) / cells]
    ).astype(np.float32)
    dft = np.stack([*as_pair(ahead), *as_pair(back)])
    return dft, phases


def small_dft(parts, sign):
    count = len(parts)
    if count == 1:
        return parts
    even = small_dft(parts[0::2], sign)
    odd = small_dft(parts[1::2], sign)
    low, high = [], []
    for k in range(count // 2):
        (er, ei), (r, i) = even[k], odd[k]
        turn = 8 * k / count
        if turn == 2:
            r, i = (-i, r) if sign > 0 else (i, -r)
        elif turn == 1:
            h = math.sqrt(0.5)
            r, i = (h * (r - sign * i), h * (i + sign * r))
        elif turn == 3:
            h = math.sqrt(0.5)
            r, i = (-h * (r + sign * i), h * (sign * r - i))
        elif k:
            c, s = math.cos(TWO_PI * k / count), sign * math.sin(TWO_PI * k / count)
            r, i = (r * c - i * s, r * s + i * c)
        low.append((er + r, ei + i))
        high.append((er - r, ei - i))
    return low + high


def product(value, dft_ref, high):
    top = value.astype(jnp.bfloat16)
    rest = (value - top.astype(jnp.float32)).astype(jnp.bfloat16)
    dot = functools.partial(jnp.dot, preferred_element_type=jnp.float32)
    return dot(top, dft_ref[high]) + (dot(top, dft_ref[high + 1]) + dot(rest, dft_ref[high]))


def chunk_pass(re, im, dft_ref, phase_ref, sign):
    lines, cells = re.shape
    outer = cells // LANES
    cut = [slice(LANES * a, LANES * (a + 1)) for a in range(outer)]
    parts = small_dft([(re[:, c], im[:, c]) for c in cut], -1)
    rows = []
    for k, (r, i) in enumerate(parts):
        c, s = phase_ref[0, k : k + 1], phase_ref[1, k : k + 1]
        rows.append(jnp.concatenate([r * c - i * s, r * s + i * c], 1))
    z = product(jnp.concatenate(rows, 0), dft_ref, 0)
    rows = []
    for k in range(outer):
        r, i = z[lines * k : lines * (k + 1), :LANES], z[lines * k : lines * (k + 1), LANES:]
        c, s = phase_ref[2, k : k + 1], sign * phase_ref[3, k : k + 1]
        rows.append(jnp.concatenate([r * c - i * s, r * s + i * c], 1))
    z = product(jnp.concatenate(rows, 0), dft_ref, 2)
    parts = []
    for k in range(outer):
        r, i = z[lines * k : lines * (k + 1), :LANES], z[lines * k : lines * (k + 1), LANES:]
        c, s = phase_ref[0, k : k + 1], phase_ref[1, k : k + 1]
        parts.append((r * c + i * s, i * c - r * s))
    parts = small_dft(parts, 1)
    return jnp.concatenate([p[0] for p in parts], 1), jnp.concatenate([p[1] for p in parts], 1)


def cos_sin(x):
    y = x * x
    c = jnp.full_like(x, 1.0 / math.factorial(16))
    for n in range(14, -1, -2):
        c = c * -y + 1.0 / math.factorial(n)
    s = jnp.full_like(x, 1.0 / math.factorial(15))
    for n in range(13, 0, -2):
        s = s * -y + 1.0 / math.factorial(n)
    return c, s * x


def mega_kernel(
    depth_count,
    screens_ref, wave_ref, target_ref, dft_ref, phase_ref,
    out_ref,
    result, kept, angle, grads, send, recv,
    send_sem, recv_sem, out_sem, in_sem, back_out_sem, back_in_sem,
):
    _, lines, cells = wave_ref.shape
    count = cells // lines
    per_tile = max(1, LANES // lines)
    depth_at, trans_at = lax.axis_index("depth"), lax.axis_index("trans")
    me = trans_at * depth_count + depth_at
    step = min(16, lines)
    stages = lines // step

    def device(at):
        return {"trans": at // depth_count, "depth": at % depth_count}

    def remote(slot, stage, to):
        return pltpu.make_async_remote_copy(
            src_ref=send.at[slot, stage, to],
            dst_ref=recv.at[slot, stage, me],
            send_sem=send_sem.at[slot],
            recv_sem=recv_sem.at[slot, stage],
            device_id=device(to),
            device_id_type=pl.DeviceIdType.MESH,
        )

    def send_to(slot, stage, to):
        @pl.when(to != me)
        def _():
            remote(slot, stage, to).start()

    def turn_start(slot, top, bottom):
        tiles = cells // LANES

        @pl.loop(0, tiles, unroll=2)
        def _(turn_at):
            tile = lax.rem(me * lines // LANES + turn_at, tiles)
            cols = pl.ds(pl.multiple_of(tile * LANES, LANES), LANES)
            block = jnp.concatenate([top[:, cols], bottom[:, cols]], 0).T
            for part in range(per_tile):
                to = tile * per_tile + part
                for stage in range(stages):
                    begin = part * lines + stage * step
                    send[slot, stage, to] = block[begin : begin + step]
                send_to(slot, 0, to)

        for stage in range(stages):
            recv[slot, stage, me] = send[slot, stage, me]

        @pl.loop(count, stages * count)
        def _(at):
            send_to(slot, at // count, lax.rem(me + at, count))

    def wait_stage(slot, stage):
        part = recv.at[slot, stage, pl.ds(0, count - 1)]
        pltpu.make_async_copy(part, part, recv_sem.at[slot, stage]).wait()

    def wait_sent(slot):
        for stage in range(stages):
            part = send.at[slot, stage, pl.ds(0, count - 1)]
            pltpu.make_async_copy(part, part, send_sem.at[slot]).wait()

    def arrived(slot, stage):
        blocks = [recv[slot, stage, at] for at in range(count)]
        return (
            jnp.concatenate([b[:, :lines] for b in blocks], 1),
            jnp.concatenate([b[:, lines:] for b in blocks], 1),
        )

    def chunks(body, unroll=False):
        @pl.loop(0, stages, unroll=unroll)
        def _(at):
            body(at, pl.ds(pl.multiple_of(at * step, step), step))

    def line_chunk(re, im, sign):
        return chunk_pass(re, im, dft_ref, phase_ref, sign)

    def screen_copy(to, owner):
        return pltpu.make_async_remote_copy(
            src_ref=screens_ref.at[0, pl.ds(to * lines, lines)],
            dst_ref=angle.at[owner],
            send_sem=out_sem.at[to],
            recv_sem=in_sem.at[owner],
            device_id={"depth": to, "trans": trans_at},
            device_id_type=pl.DeviceIdType.MESH,
        )

    def grad_copy(to, owner, begin, size):
        rows = pl.ds(pl.multiple_of(owner * lines + begin, size), size)
        return pltpu.make_async_remote_copy(
            src_ref=grads.at[to, pl.ds(begin, size)],
            dst_ref=out_ref.at[0, rows],
            send_sem=back_out_sem.at[to],
            recv_sem=back_in_sem.at[owner],
            device_id={"depth": to, "trans": trans_at},
            device_id_type=pl.DeviceIdType.MESH,
        )

    def grad_start(to, at):
        begin = pl.multiple_of(at * step, step)

        @pl.when(depth_at != to)
        def _():
            grad_copy(to, depth_at, begin, step).start()

        @pl.when(depth_at == to)
        def _():
            out_ref[0, pl.ds(to * lines + begin, step)] = grads[to, pl.ds(begin, step)]

    barrier = pltpu.get_barrier_semaphore()

    @pl.loop(0, count)
    def _(at):
        @pl.when(at != me)
        def _():
            pl.semaphore_signal(
                barrier, inc=1, device_id=device(at), device_id_type=pl.DeviceIdType.MESH
            )

    pl.semaphore_wait(barrier, count - 1)

    for to in range(depth_count):
        @pl.when(depth_at != to)
        def _():
            screen_copy(to, depth_at).start()

        @pl.when(depth_at == to)
        def _():
            angle[to] = screens_ref[0, pl.ds(to * lines, lines)]

    for to in range(depth_count):
        @pl.when(depth_at != to)
        def _():
            screen_copy(to, to).wait_recv()
            screen_copy(to, to).wait_send()

    turn_start(2, angle.at[1], angle.at[3])

    def enter(g, r, i, here):
        c, s = cos_sin(angle[g, here])
        r, i = r * c - i * s, r * s + i * c
        kept[g, 0, here] = r
        kept[g, 1, here] = i
        result[0, here], result[1, here] = line_chunk(r, i, 1.0)

    def leave(g, r, i, here):
        grads[g, here] = i * kept[g, 0, here] - r * kept[g, 1, here]

    def first(at, here):
        enter(0, wave_ref[0, here], wave_ref[1, here], here)

    chunks(first, True)
    turn_start(0, result.at[0], result.at[1])

    def unpack_screens(at, here):
        wait_stage(2, at)
        angle[1, here], angle[3, here] = arrived(2, at)

    chunks(unpack_screens)
    wait_sent(2)

    @pl.loop(1, depth_count)
    def _(g):
        slot = (g - 1) % 2

        def body(at, here):
            wait_stage(slot, at)
            r, i = line_chunk(*arrived(slot, at), 1.0)
            enter(g, r, i, here)

        chunks(body)
        wait_sent(slot)
        turn_start(g % 2, result.at[0], result.at[1])

    last = (depth_count - 1) % 2

    def residual(at, here):
        wait_stage(last, at)
        r, i = line_chunk(*arrived(last, at), 1.0)
        r, i = r - target_ref[0, here], i - target_ref[1, here]
        result[0, here], result[1, here] = line_chunk(r, i, -1.0)

    chunks(residual)
    wait_sent(last)
    turn_start(1 - last, result.at[0], result.at[1])

    @pl.loop(1, depth_count)
    def _(turned):
        g = depth_count - turned
        slot = (last + turned) % 2

        def body(at, here):
            wait_stage(slot, at)
            r, i = line_chunk(*arrived(slot, at), -1.0)
            leave(g, r, i, here)
            c, s = cos_sin(angle[g, here])
            r, i = r * c + i * s, i * c - r * s
            result[0, here], result[1, here] = line_chunk(r, i, -1.0)

            @pl.when(g == 2)
            def _():
                grad_start(2, at)

        chunks(body)
        wait_sent(slot)

        @pl.when(g == 1)
        def _():
            turn_start(3, grads.at[1], grads.at[3])

        turn_start(1 - slot, result.at[0], result.at[1])

    def unpack_grads(at, here):
        wait_stage(3, at)
        grads[1, here], grads[3, here] = arrived(3, at)
        grad_start(1, at)
        grad_start(3, at)

    chunks(unpack_grads)
    wait_sent(3)
    slot = (last + depth_count) % 2

    def final(at, here):
        wait_stage(slot, at)
        r, i = line_chunk(*arrived(slot, at), -1.0)
        leave(0, r, i, here)
        grad_start(0, at)

    chunks(final)
    wait_sent(slot)
    for to in range(depth_count):
        @pl.when(depth_at != to)
        def _():
            grad_copy(to, to, 0, lines).wait_recv()
            grad_copy(to, to, 0, lines).wait_send()


def whole_chain(screens, wave, target, tables, depth_count):
    two, lines, cells = wave.shape
    count = cells // lines
    step = min(16, lines)
    stages = lines // step
    f32 = jnp.float32
    whole = pl.BlockSpec(memory_space=pltpu.VMEM)
    return pl.pallas_call(
        functools.partial(mega_kernel, depth_count),
        out_shape=jax.ShapeDtypeStruct(screens.shape, f32),
        in_specs=[whole] * 5,
        out_specs=whole,
        scratch_shapes=[
            pltpu.VMEM((two, lines, cells), f32),
            pltpu.VMEM((depth_count, two, lines, cells), f32),
            pltpu.VMEM((depth_count, lines, cells), f32),
            pltpu.VMEM((depth_count, lines, cells), f32),
            pltpu.VMEM((4, stages, count, step, two * lines), f32),
            pltpu.VMEM((4, stages, count, step, two * lines), f32),
            pltpu.SemaphoreType.DMA((4,)),
            pltpu.SemaphoreType.DMA((4, stages)),
            pltpu.SemaphoreType.DMA((depth_count,)),
            pltpu.SemaphoreType.DMA((depth_count,)),
            pltpu.SemaphoreType.DMA((depth_count,)),
            pltpu.SemaphoreType.DMA((depth_count,)),
        ],
        compiler_params=pltpu.CompilerParams(
            collective_id=0, has_side_effects=True, vmem_limit_bytes=56 << 20
        ),
        name="whole_chain",
    )(screens, wave, target, *tables)


def illumination(angle_index, first, lines, cells):
    def wave(positions, tilt):
        turns = lax.rem(lax.rem(positions * tilt, cells) + cells, cells)
        radians = TWO_PI / cells * turns.astype(jnp.float32)
        return jnp.cos(radians), jnp.sin(radians)

    column = wave(jnp.arange(cells, dtype=jnp.int32), angle_index[0, 0])
    row = wave(first + jnp.arange(lines, dtype=jnp.int32), angle_index[0, 1])
    cc, cs = column[0][None], column[1][None]
    rc, rs = row[0][:, None], row[1][:, None]
    return jnp.stack((cc * rc - cs * rs, cc * rs + cs * rc))


def on_device(screens, measured, angle_index):
    depth_count = lax.axis_size("depth")
    held, cells = screens.shape[1:]
    lines = held // depth_count
    depth_at = lax.axis_index("depth")
    first = lax.axis_index("trans") * held + depth_at * lines
    tables = [jnp.asarray(t) for t in tables_of(cells)]

    wave = illumination(angle_index, first, lines, cells)
    target = lax.dynamic_slice_in_dim(measured[0], depth_at * lines, lines, 1)
    return whole_chain(screens, wave, target.astype(jnp.float32), tables, depth_count)


def solution(mesh):
    placed = (P("depth", "trans", None), P(None, None, "trans", None), P())
    return jax.shard_map(
        on_device, mesh=mesh, in_specs=placed, out_specs=P("depth", "trans", None), check_vma=False
    )
```
